256 devices in a mesh: tm: 16 (over x, z_hi, core), win: 4 (over z_lo), space: 4 (over y).
Axes of the slice: x: 4, y: 4, z: 8 (z_hi: 2, z_lo: 4; z = z_hi * 4 + z_lo), core: 2. Of those that a mesh axis runs over, the one named last changes fastest.
Arguments:
- states: float32 [4, 16, 3, 256, 2048], P('win', 'tm', None, 'space'), may hold values from -4 to 4
- initial_state: float32 [3, 256, 2048], P(None, 'space'), may hold values from -4 to 4
Outputs:
- coeffs: float32 [4, 9, 256, 2048], P('win', None, 'space')
- residual: float32 [4, 16, 3, 256, 2048], P('win', 'tm', None, 'space')
The draws below stay inside these ranges and needn't reach their ends.
All inputs are finite; a program needn't handle non-finite values.
Results may differ from the reference program's by a relative error of at most 0.00002.
Values sent between devices are 32-bit elements; how exact they have to be, the bound alone decides.
No kernel may reach another device: no remote copies, remote signals or barrier semaphores. Data moves between devices by JAX's collectives and lax.ppermute only.
A program may use at most 64 MiB of HBM per device.

```python
import jax
import jax.numpy as jnp
from jax import lax

COLS = 2048
NX = 256
STEPS = 16
NWIN = 4


def steps_of(stream_key, dims, pieces, least, high):
    def one(axis_at, blocks):
        steps = jax.random.uniform(jax.random.fold_in(jax.random.fold_in(stream_key, 6), axis_at), (blocks,), jnp.float32, least / len(pieces), high / len(pieces))
        return jnp.repeat(jnp.exp(steps), dims[axis_at] // blocks).reshape((-1,) + (1,) * (len(dims) - axis_at - 1))

    factor_of = one(*pieces[0])
    for cut in pieces[1:]:
        factor_of = factor_of * one(*cut)
    return factor_of


def noise(key, extent, deviation, most, cuts=(), dtype=jnp.bfloat16):
    values = deviation * jax.random.normal(key, extent, jnp.float32)
    if cuts:
        values = values * steps_of(key, extent, cuts, -0.22, 0.18)
    return jnp.clip(values, -most, most).astype(dtype)


def setup_inputs(seed: int = 0) -> dict:
    seeds = jax.random.split(jax.random.key(seed), 3)
    states = noise(seeds[0], (NWIN, STEPS, 3, NX, COLS), 0.5, 4.0, ((0, 4), (1, 16), (3, 4)), jnp.float32)
    initial_state = noise(seeds[1], (3, NX, COLS), 0.5, 4.0, ((1, 4),), jnp.float32)
    return dict(states=states, initial_state=initial_state)


mean_depth = 1.0
coriolis_rate = 1.0
grav_accel = 1.0
time_step = 0.5


def coeff_fields(state):
    ddx = (jnp.roll(state, -1, -1) - jnp.roll(state, 1, -1)) * 0.5
    ddy = (jnp.roll(state, -1, -2) - jnp.roll(state, 1, -2)) * 0.5
    speed_u = state[..., 0, :, :]
    speed_v = state[..., 1, :, :]
    depth = mean_depth + state[..., 2, :, :]
    return jnp.stack([speed_u, speed_v, depth, ddx[..., 0, :, :], ddy[..., 0, :, :], ddx[..., 1, :, :], ddy[..., 1, :, :], ddx[..., 2, :, :], ddy[..., 2, :, :]], axis=-3)


def tendency(fields):
    speed_u, speed_v, depth = fields[..., 0, :, :], fields[..., 1, :, :], fields[..., 2, :, :]
    u_dx, u_dy, v_dx, v_dy = fields[..., 3, :, :], fields[..., 4, :, :], fields[..., 5, :, :], fields[..., 6, :, :]
    e_dx, e_dy = fields[..., 7, :, :], fields[..., 8, :, :]
    force_u = -speed_u * u_dx - speed_v * u_dy + coriolis_rate * speed_v - grav_accel * e_dx
    force_v = -speed_u * v_dx - speed_v * v_dy - coriolis_rate * speed_u - grav_accel * e_dy
    force_e = -(depth * u_dx + speed_u * e_dx) - (depth * v_dy + speed_v * e_dy)
    return jnp.stack([force_u, force_v, force_e], axis=-3)


def reference(states, initial_state):
    flat = states.reshape((NWIN * STEPS, 3, NX, COLS))
    before = jnp.concatenate([initial_state[None], flat[:-1]], axis=0).reshape(states.shape)

    def per_window(pair):
        window, earlier = pair
        fields = coeff_fields(window)
        averaged = jnp.sum(fields, axis=0) / STEPS
        left = window - earlier - time_step * tendency(fields)
        return averaged, left

    coeffs, residual = lax.map(per_window, (states, before))
    return coeffs, residual
```

```python
import jax
import jax.numpy as jnp
from jax import lax
from jax.experimental import pallas as pl
from jax.experimental.pallas import tpu as pltpu
from jax.sharding import PartitionSpec as P

AXES = ("tm", "win", "space")
VMEM_BYTES = 24 * 1024 * 1024


def place(x, z, y, core):
    z_hi, z_lo = divmod(z % 8, 4)
    tm = ((x % 4) * 2 + z_hi) * 2 + core
    return (tm * 4 + z_lo) * 4 + y % 4


def pairs(target):
    found = []
    for x in range(4):
        for z in range(8):
            for y in range(4):
                for core in range(2):
                    to = target(x, z, y, core)
                    if to is not None:
                        found.append((place(x, z, y, core), place(*to)))
    return found


def send(value, target):
    return lax.ppermute(value, AXES, pairs(target))


def step_target(x, z, y, core):
    if core == 0:
        return None
    if z < 4:
        return (x, z + 4, y, 0)
    if x < 3:
        return (x + 1, z - 4, y, 0)
    return {4: (0, 1, y, 0), 5: (3, 7, y, 1), 6: (0, 3, y, 0), 7: None}[z]


def relay_target(x, z, y, core):
    return (0, 2, y, 0) if (x, z, core) == (3, 7, 1) else None


def swap_target(x, z, y, core):
    return (x, z, y, 1 - core)


def x_target(by):
    return lambda x, z, y, core: (x + by, z, y, core)


def z_target(x, z, y, core):
    return (x, z + 4, y, core)


def up_target(x, z, y, core):
    return (x, z, y + 1, core)


def down_target(x, z, y, core):
    return (x, z, y - 1, core)


def edge_target(flip):
    def target(x, z, y, core):
        return (x, z, y - 1 if core == 0 else y + 1, core ^ flip)

    return target


def params():
    return pltpu.CompilerParams(vmem_limit_bytes=VMEM_BYTES)


def ddx(value):
    width = value.shape[1]
    return (pltpu.roll(value, width - 1, 1) - pltpu.roll(value, 1, 1)) * 0.5


def ddy(above, value, below):
    row = lax.broadcasted_iota(jnp.int32, value.shape, 0)
    after = jnp.where(row == 7, pltpu.roll(below, 7, 0), pltpu.roll(value, 7, 0))
    before = jnp.where(row == 0, pltpu.roll(above, 1, 0), pltpu.roll(value, 1, 0))
    return (after - before) * 0.5


def split_kernel(where_ref, *refs):
    for k in range(4):
        refs[8 + k][...] = (refs[k][...] + refs[4 + k][...])[:, 0]


def split_sum(where, own, other):
    own, other = (a.reshape(3, 8, 8, -1) for a in (own, other))
    cols = own.shape[-1]

    def spec(k):
        return pl.BlockSpec((3, 1, 8, cols), lambda i, w: (0, w[1] * 4 + (w[0] + k) % 4, 0, 0))

    piece = pl.BlockSpec((3, 8, cols), lambda i, w: (0, 0, 0))
    return pl.pallas_call(
        split_kernel,
        grid_spec=pltpu.PrefetchScalarGridSpec(
            num_scalar_prefetch=1,
            grid=(1,),
            in_specs=[spec(k) for k in range(4)] * 2,
            out_specs=[piece] * 4,
        ),
        out_shape=[jax.ShapeDtypeStruct((3, 8, cols), jnp.float32)] * 4,
        compiler_params=params(),
        name="split_sum",
    )(where, *([own] * 4), *([other] * 4))


def gather_kernel(where_ref, p0, p1, p2, p3, half_ref, edge_ref):
    x, core = where_ref[0], where_ref[1]
    for k, piece in enumerate((p0, p1, p2, p3)):
        slot = (x + k) % 4
        half_ref[:, slot] = piece[...]

        @pl.when((core == 0) & (slot == 0))
        def _():
            edge_ref[...] = piece[:, 0:1]

        @pl.when((core == 1) & (slot == 3))
        def _():
            edge_ref[...] = piece[:, 7:8]


def gather(where, pieces):
    cols = pieces[0].shape[-1]
    vmem = pl.BlockSpec(memory_space=pltpu.VMEM)
    return pl.pallas_call(
        gather_kernel,
        in_specs=[pl.BlockSpec(memory_space=pltpu.SMEM)] + [vmem] * 4,
        out_specs=[vmem] * 2,
        out_shape=[
            jax.ShapeDtypeStruct((3, 4, 8, cols), jnp.float32),
            jax.ShapeDtypeStruct((3, 1, cols), jnp.float32),
        ],
        compiler_params=params(),
        name="gather",
    )(where, *pieces)


def coeffs_kernel(where_ref, half_ref, other_ref, near_ref, far_ref, out_ref, mean):
    step = pl.program_id(0)

    @pl.when(step == 0)
    def _():
        core = where_ref[1]
        mean[:, pl.ds(1 + core * 4, 4)] = half_ref[...]
        mean[:, pl.ds(5 - core * 4, 4)] = other_ref[...]

        @pl.when(core == 0)
        def _():
            mean[:, 9, 0:1] = near_ref[...]
            mean[:, 0, 7:8] = far_ref[...]

        @pl.when(core == 1)
        def _():
            mean[:, 0, 7:8] = near_ref[...]
            mean[:, 9, 0:1] = far_ref[...]

    for f in range(3):
        value = mean[f, step + 1]
        out_ref[f] = value + 1.0 if f == 2 else value
        out_ref[3 + 2 * f] = ddx(value)
        out_ref[4 + 2 * f] = ddy(mean[f, step], value, mean[f, step + 2])


def coeffs_of(where, half, other, near, far):
    cols = half.shape[-1]

    def whole(a):
        return pl.BlockSpec(a.shape, lambda i, w: (0,) * a.ndim)

    return pl.pallas_call(
        coeffs_kernel,
        grid_spec=pltpu.PrefetchScalarGridSpec(
            num_scalar_prefetch=1,
            grid=(8,),
            in_specs=[whole(a) for a in (half, other, near, far)],
            out_specs=pl.BlockSpec((9, 8, cols), lambda i, w: (0, i, 0)),
            scratch_shapes=[pltpu.VMEM((3, 10, 8, cols), jnp.float32)],
        ),
        out_shape=jax.ShapeDtypeStruct((9, 64, cols), jnp.float32),
        compiler_params=params(),
        name="coeffs",
    )(where, half, other, near, far)


def local_kernel(state_ref, above_ref, below_ref, out_ref):
    def block(f, r):
        if r < 0:
            return jnp.broadcast_to(above_ref[f], (8, above_ref.shape[-1]))
        if r > 7:
            return jnp.broadcast_to(below_ref[f], (8, below_ref.shape[-1]))
        return state_ref[f, r]

    for r in range(8):
        u, v, e = (state_ref[f, r] for f in range(3))
        dx = [ddx(w) for w in (u, v, e)]
        dy = [ddy(block(f, r - 1), w, block(f, r + 1)) for f, w in enumerate((u, v, e))]
        force_u = -u * dx[0] - v * dy[0] + v - dx[2]
        force_v = -u * dx[1] - v * dy[1] - u - dy[2]
        depth = 1.0 + e
        force_e = -(depth * dx[0] + u * dx[2]) - (depth * dy[1] + v * dy[2])
        out_ref[0, r] = u - 0.5 * force_u
        out_ref[1, r] = v - 0.5 * force_v
        out_ref[2, r] = e - 0.5 * force_e


def local_part(state, above, below):
    cols = state.shape[-1]
    vmem = pl.BlockSpec(memory_space=pltpu.VMEM)
    return pl.pallas_call(
        local_kernel,
        in_specs=[vmem] * 3,
        out_specs=vmem,
        out_shape=jax.ShapeDtypeStruct((3, 8, 8, cols), jnp.float32),
        compiler_params=params(),
        name="local_part",
    )(state.reshape(3, 8, 8, cols), above, below)


def residual_kernel(which_ref, local_ref, *refs):
    out_ref = refs[-1]
    for k, previous in enumerate(refs[:-1]):

        @pl.when(which_ref[0] == k)
        def _():
            out_ref[...] = local_ref[...] - previous[...]


def residual_of(which, local, candidates):
    cols = local.shape[-1]

    def spec(k):
        return pl.BlockSpec((1, 64, cols), lambda i, w: (jnp.where(w[0] == k, i, 0), 0, 0))

    block = pl.BlockSpec((1, 64, cols), lambda i, w: (i, 0, 0))
    return pl.pallas_call(
        residual_kernel,
        grid_spec=pltpu.PrefetchScalarGridSpec(
            num_scalar_prefetch=1,
            grid=(3,),
            in_specs=[block] + [spec(k) for k in range(len(candidates))],
            out_specs=block,
        ),
        out_shape=jax.ShapeDtypeStruct((3, 64, cols), jnp.float32),
        compiler_params=params(),
        name="residual",
    )(which, local, *candidates)


def shards(states, initial_state):
    current = states[0, 0]
    cols = current.shape[-1]
    step, window = lax.axis_index("tm"), lax.axis_index("win")
    x, core = step // 4, step % 2
    where = jnp.stack([x, core]).astype(jnp.int32)

    other = send(current, swap_target)
    far = send(current, step_target)
    above = send(current[:, 63:64], up_target)
    below = send(current[:, 0:1], down_target)

    pieces = split_sum(where, current, other)
    came = [send(pieces[k], x_target(k)) for k in (1, 3, 2)]
    part = (pieces[0] + came[0]) + (came[1] + came[2])
    part = (part + send(part, z_target)) * (1.0 / 16.0)
    gathered = [part] + [send(part, x_target(-k)) for k in (1, 2, 3)]
    half, edge = gather(where, gathered)
    other_half = send(half, swap_target)
    near = send(edge, edge_target(0))
    beyond = send(edge, edge_target(1))
    coeffs = coeffs_of(where, half, other_half, near, beyond)

    local = local_part(current, above, below).reshape(3, 64, cols)
    relayed = send(far, relay_target)
    first = jnp.where(window == 0, 3, jnp.where(window == 2, 2, 1))
    which = jnp.where(core == 1, 0, jnp.where(step == 0, first, 1)).astype(jnp.int32).reshape(1)
    residual = residual_of(which, local, (other, far, relayed, initial_state))
    return coeffs[None], residual[None, None]


def solution(mesh):
    in_specs = (P("win", "tm", None, "space", None), P(None, "space", None))
    out_specs = (P("win", None, "space", None), P("win", "tm", None, "space", None))
    return jax.shard_map(shards, mesh=mesh, in_specs=in_specs, out_specs=out_specs, check_vma=False)
```

```python
import jax
import jax.numpy as jnp
from jax import lax
from jax.experimental import pallas as pl
from jax.experimental.pallas import tpu as pltpu
from jax.sharding import PartitionSpec as P

AXES = ("tm", "win", "space")
VMEM_BYTES = 12 * 1024 * 1024
WHOLE = pl.BlockSpec(memory_space=pltpu.VMEM)
SCALARS = pl.BlockSpec(memory_space=pltpu.SMEM)


def place(x, z, y, core):
    z_hi, z_lo = divmod(z % 8, 4)
    tm = ((x % 4) * 2 + z_hi) * 2 + core
    return (tm * 4 + z_lo) * 4 + y % 4


def pairs(target):
    found = []
    for x in range(4):
        for z in range(8):
            for y in range(4):
                for core in range(2):
                    to = target(x, z, y, core)
                    if to is not None:
                        found.append((place(x, z, y, core), place(*to)))
    return found


def send(value, target):
    return lax.ppermute(value, AXES, pairs(target))


def cross_first(x, z, y, core):
    if core == 0 or (x, z) == (3, 7):
        return None
    return (x, z + 4, y, 0) if z < 4 else (x, z - 4, y, 1)


def step_last(x, z, y, core):
    if core == 0 or z > 3:
        return None
    if x < 3:
        return (x + 1, z, y, 0)
    return (0, z + 1, y, 0) if z < 3 else None


def step_first(x, z, y, core):
    if core == 0 or z < 4:
        return None
    if x < 3:
        return (x + 1, z, y, 1)
    return (0, z + 1, y, 1) if z < 7 else None


def cross_last(x, z, y, core):
    return (x, z + 4, y, 0) if core == 1 else None


def swap_target(x, z, y, core):
    return (x, z, y, 1 - core)


def after(value, *others):
    return lax.optimization_barrier((value,) + others)[0]


def x_target(by):
    return lambda x, z, y, core: (x + by, z, y, core)


def z_target(x, z, y, core):
    return (x, z + 4, y, core)


def up_target(x, z, y, core):
    return (x, z, y + 1, core)


def down_target(x, z, y, core):
    return (x, z, y - 1, core)


def edge_target(flip):
    def target(x, z, y, core):
        return (x, z, y - 1 if core == 0 else y + 1, core ^ flip)

    return target


def call(kernel, out_shape, *operands, **options):
    return pl.pallas_call(
        kernel,
        out_shape=out_shape,
        compiler_params=pltpu.CompilerParams(vmem_limit_bytes=VMEM_BYTES),
        cost_estimate=pl.CostEstimate(flops=1, bytes_accessed=1, transcendentals=0),
        **options,
    )(*operands)


def in_vmem(value):
    return pltpu.with_memory_space_constraint(value, pltpu.VMEM)


def vmem_out(*shape):
    return pltpu.VMEM(shape, jnp.float32)


def ddx(value):
    width = value.shape[1]
    return (pltpu.roll(value, width - 1, 1) - pltpu.roll(value, 1, 1)) * 0.5


def ddy(above, value, below):
    row = lax.broadcasted_iota(jnp.int32, value.shape, 0)
    after = jnp.where(row == 7, pltpu.roll(below, 7, 0), pltpu.roll(value, 7, 0))
    before = jnp.where(row == 0, pltpu.roll(above, 1, 0), pltpu.roll(value, 1, 0))
    return (after - before) * 0.5


def split_kernel(where_ref, own_ref, other_ref, *out_refs):
    x, core = where_ref[0], where_ref[1]
    for k, out_ref in enumerate(out_refs):
        block = core * 4 + (x + k) % 4
        out_ref[...] = own_ref[:, block] + other_ref[:, block]


def split_sum(where, own, other):
    cols = own.shape[-1]
    own, other = (a.reshape(3, 8, 8, cols) for a in (own, other))
    return call(
        split_kernel,
        [vmem_out(3, 8, cols)] * 4,
        where,
        in_vmem(own),
        in_vmem(other),
        in_specs=[SCALARS, WHOLE, WHOLE],
        out_specs=[WHOLE] * 4,
        name="split_sum",
    )


def edge_kernel(where_ref, p0, p1, p2, p3, edge_ref):
    x, core = where_ref[0], where_ref[1]
    for k, piece in enumerate((p0, p1, p2, p3)):
        slot = (x + k) % 4

        @pl.when((core == 0) & (slot == 0))
        def _():
            edge_ref[...] = piece[:, 0:1]

        @pl.when((core == 1) & (slot == 3))
        def _():
            edge_ref[...] = piece[:, 7:8]


def edge_of(where, pieces):
    cols = pieces[0].shape[-1]
    return call(
        edge_kernel,
        vmem_out(3, 1, cols),
        where,
        *map(in_vmem, pieces),
        in_specs=[SCALARS] + [WHOLE] * 4,
        out_specs=WHOLE,
        name="edge",
    )


def coeffs_kernel(where_ref, *refs):
    near_ref, far_ref, out_ref, mean, fields, sems = refs[8:]
    x, core = where_ref[0], where_ref[1]
    for k in range(4):
        slot = (x + k) % 4
        mean[:, 1 + core * 4 + slot] = refs[k][...]
        mean[:, 5 - core * 4 + slot] = refs[4 + k][...]

    @pl.when(core == 0)
    def _():
        mean[:, 9, 0:1] = near_ref[...]
        mean[:, 0, 7:8] = far_ref[...]

    @pl.when(core == 1)
    def _():
        mean[:, 0, 7:8] = near_ref[...]
        mean[:, 9, 0:1] = far_ref[...]

    copies = []
    for part in range(4):
        rows = pl.ds(part * 16, 16)
        for f in range(3):
            for r in (2 * part, 2 * part + 1):
                value = mean[f, r + 1]
                block = pl.ds(r * 8, 8)
                fields[f, block] = value + 1.0 if f == 2 else value
                fields[3 + 2 * f, block] = ddx(value)
                fields[4 + 2 * f, block] = ddy(mean[f, r], value, mean[f, r + 2])
            for planes in (pl.ds(f, 1), pl.ds(3 + 2 * f, 2)):
                copy = pltpu.make_async_copy(fields.at[planes, rows], out_ref.at[planes, rows], sems.at[len(copies)])
                copy.start()
                copies.append(copy)
    for copy in copies:
        copy.wait()


def coeffs_of(where, pieces, others, near, far):
    cols = near.shape[-1]
    return call(
        coeffs_kernel,
        jax.ShapeDtypeStruct((9, 64, cols), jnp.float32),
        where,
        *map(in_vmem, (*pieces, *others, near, far)),
        in_specs=[SCALARS] + [WHOLE] * 10,
        out_specs=pl.BlockSpec(memory_space=pl.ANY),
        scratch_shapes=[
            pltpu.VMEM((3, 10, 8, cols), jnp.float32),
            pltpu.VMEM((9, 64, cols), jnp.float32),
            pltpu.SemaphoreType.DMA((24,)),
        ],
        name="coeffs",
    )


def stage_kernel(state_ref, out_ref):
    out_ref[...] = state_ref[...]


def stage(state):
    return call(stage_kernel, vmem_out(*state.shape), state, in_specs=[WHOLE], out_specs=WHOLE, name="stage")


def local_kernel(which_ref, state_ref, above_ref, below_ref, other_ref, initial_ref, out_ref):
    def block(f, r):
        if r < 0:
            return jnp.broadcast_to(above_ref[f], (8, above_ref.shape[-1]))
        if r > 7:
            return jnp.broadcast_to(below_ref[f], (8, below_ref.shape[-1]))
        return state_ref[f, r]

    for r in range(8):
        u, v, e = (state_ref[f, r] for f in range(3))
        dx = [ddx(w) for w in (u, v, e)]
        dy = [ddy(block(f, r - 1), w, block(f, r + 1)) for f, w in enumerate((u, v, e))]
        force_u = -u * dx[0] - v * dy[0] + v - dx[2]
        force_v = -u * dx[1] - v * dy[1] - u - dy[2]
        depth = 1.0 + e
        force_e = -(depth * dx[0] + u * dx[2]) - (depth * dy[1] + v * dy[2])
        out_ref[0, r] = u - 0.5 * force_u
        out_ref[1, r] = v - 0.5 * force_v
        out_ref[2, r] = e - 0.5 * force_e

    @pl.when(which_ref[0] == 1)
    def _():
        out_ref[...] = out_ref[...] - other_ref[...]

    @pl.when(which_ref[0] == 2)
    def _():
        out_ref[...] = out_ref[...] - initial_ref[...]


def local_part(which, state, above, below, other, initial):
    cols = state.shape[-1]
    state, other, initial = (a.reshape(3, 8, 8, cols) for a in (state, other, initial))
    return call(
        local_kernel,
        vmem_out(3, 8, 8, cols),
        which,
        *map(in_vmem, (state, above, below, other, initial)),
        in_specs=[SCALARS] + [WHOLE] * 5,
        out_specs=WHOLE,
        name="local_part",
    ).reshape(3, 64, cols)


def residual_kernel(core_ref, local_ref, crossed_ref, stepped_ref, second_ref, out_ref, left, sems):
    first, second = slice(0, 32), slice(32, 64)
    left[:, first] = local_ref[:, first] - stepped_ref[...]

    @pl.when(core_ref[0] == 0)
    def _():
        left[:, first] = left[:, first] - crossed_ref[...]

    copies = [pltpu.make_async_copy(left.at[:, first], out_ref.at[:, first], sems.at[0])]
    copies[0].start()
    left[:, second] = local_ref[:, second] - second_ref[...]
    copies.append(pltpu.make_async_copy(left.at[:, second], out_ref.at[:, second], sems.at[1]))
    copies[1].start()
    for copy in copies:
        copy.wait()


def residual_of(core, local, crossed, stepped, second):
    return call(
        residual_kernel,
        jax.ShapeDtypeStruct(local.shape, jnp.float32),
        core,
        *map(in_vmem, (local, crossed, stepped, second)),
        in_specs=[SCALARS] + [WHOLE] * 4,
        out_specs=pl.BlockSpec(memory_space=pl.ANY),
        scratch_shapes=[pltpu.VMEM(local.shape, jnp.float32), pltpu.SemaphoreType.DMA((2,))],
        name="residual",
    )


def shards(states, initial_state):
    current = states[0, 0]
    step, window = lax.axis_index("tm"), lax.axis_index("win")
    x, z_hi, core = step // 4, step // 2 % 2, step % 2
    where = jnp.stack([x, core]).astype(jnp.int32)

    other = send(current, swap_target)
    crossed = send(current[:, :32], cross_first)
    held = stage(current)

    pieces = split_sum(where, held, other)
    above = send(after(held, pieces[0])[:, 63:64], up_target)
    below = send(after(held, pieces[0])[:, 0:1], down_target)
    came = [send(pieces[k], x_target(k)) for k in (1, 3, 2)]
    part = (pieces[0] + came[0]) + (came[1] + came[2])

    second_half = after(held, part)[:, 32:]
    shifted = send(second_half, step_first)
    stepped = send(after(crossed, part), step_last)
    which = jnp.where(core == 1, 1, jnp.where((step == 0) & (window == 0), 2, 0)).astype(jnp.int32).reshape(1)
    local = local_part(which, after(held, part), above, below, other, initial_state)

    part = (part + after(send(part, z_target), crossed, shifted, local)) * (1.0 / 16.0)
    second = send(after(jnp.where(z_hi == 0, second_half, shifted), part), cross_last)
    gathered = [part] + [send(part, x_target(-k)) for k in (1, 2, 3)]
    others = [send(piece, swap_target) for piece in gathered]
    edge = edge_of(where, gathered)
    near = send(edge, edge_target(0))
    beyond = send(edge, edge_target(1))
    coeffs = coeffs_of(where, gathered, others, near, beyond)

    local = after(local, coeffs)
    residual = residual_of(core.astype(jnp.int32).reshape(1), local, crossed, stepped, second)
    return coeffs[None], residual[None, None]


def solution(mesh):
    in_specs = (P("win", "tm", None, "space", None), P(None, "space", None))
    out_specs = (P("win", None, "space", None), P("win", "tm", None, "space", None))
    return jax.shard_map(shards, mesh=mesh, in_specs=in_specs, out_specs=out_specs, check_vma=False)
```

```python
import jax
import jax.numpy as jnp
from jax import lax
from jax.experimental import pallas as pl
from jax.experimental.pallas import tpu as pltpu
from jax.sharding import PartitionSpec as P

AXES = ("tm", "win", "space")
VMEM_BYTES = 8 * 1024 * 1024
FIRST = 24
WHOLE = pl.BlockSpec(memory_space=pltpu.VMEM)
SCALARS = pl.BlockSpec(memory_space=pltpu.SMEM)


def place(x, z, y, core):
    z_hi, z_lo = divmod(z % 8, 4)
    tm = ((x % 4) * 2 + z_hi) * 2 + core
    return (tm * 4 + z_lo) * 4 + y % 4


def pairs(target):
    found = []
    for x in range(4):
        for z in range(8):
            for y in range(4):
                for core in range(2):
                    to = target(x, z, y, core)
                    if to is not None:
                        found.append((place(x, z, y, core), place(*to)))
    return found


def send(value, target):
    return lax.ppermute(value, AXES, pairs(target))


def cross_first(x, z, y, core):
    if core == 0 or (x, z) == (3, 7):
        return None
    return (x, z + 4, y, 0) if z < 4 else (x, z - 4, y, 1)


def step_last(x, z, y, core):
    if core == 0 or z > 3:
        return None
    if x < 3:
        return (x + 1, z, y, 0)
    return (0, z + 1, y, 0) if z < 3 else None


def step_first(x, z, y, core):
    if core == 0 or z < 4:
        return None
    if x < 3:
        return (x + 1, z, y, 1)
    return (0, z + 1, y, 1) if z < 7 else None


def cross_last(x, z, y, core):
    return (x, z + 4, y, 0) if core == 1 else None


def swap_target(x, z, y, core):
    return (x, z, y, 1 - core)


def after(value, *others):
    return lax.optimization_barrier((value,) + others)[0]


def x_target(by):
    return lambda x, z, y, core: (x + by, z, y, core)


def z_target(x, z, y, core):
    return (x, z + 4, y, core)


def up_target(x, z, y, core):
    return (x, z, y + 1, core)


def down_target(x, z, y, core):
    return (x, z, y - 1, core)


def edge_target(x, z, y, core):
    if (x, core) == (0, 0):
        return (x, z, y - 1, core)
    return (x, z, y + 1, core) if (x, core) == (3, 1) else None


def call(kernel, out_shape, *operands, **options):
    return pl.pallas_call(
        kernel,
        out_shape=out_shape,
        compiler_params=pltpu.CompilerParams(vmem_limit_bytes=VMEM_BYTES),
        cost_estimate=pl.CostEstimate(flops=1, bytes_accessed=1, transcendentals=0),
        **options,
    )(*operands)


def in_vmem(value):
    return pltpu.with_memory_space_constraint(value, pltpu.VMEM)


def vmem_out(*shape):
    return pltpu.VMEM(shape, jnp.float32)


def ddx(value):
    width = value.shape[1]
    return (pltpu.roll(value, width - 1, 1) - pltpu.roll(value, 1, 1)) * 0.5


def ddy(above, value, below):
    row = lax.broadcasted_iota(jnp.int32, value.shape, 0)
    after = jnp.where(row == 7, pltpu.roll(below, 7, 0), pltpu.roll(value, 7, 0))
    before = jnp.where(row == 0, pltpu.roll(above, 1, 0), pltpu.roll(value, 1, 0))
    return (after - before) * 0.5


def split_kernel(where_ref, own_ref, other_ref, *out_refs):
    x, core = where_ref[0], where_ref[1]
    for k, out_ref in enumerate(out_refs):
        block = core * 4 + (x + k) % 4
        out_ref[...] = own_ref[:, block] + other_ref[:, block]


def split_sum(where, own, other):
    cols = own.shape[-1]
    own, other = (a.reshape(3, 8, 8, cols) for a in (own, other))
    return call(
        split_kernel,
        [vmem_out(3, 8, cols)] * 4,
        where,
        in_vmem(own),
        in_vmem(other),
        in_specs=[SCALARS, WHOLE, WHOLE],
        out_specs=[WHOLE] * 4,
        name="split_sum",
    )


def pack_kernel(part_ref, edge_ref, out_ref):
    for f in range(3):
        for t in range(8):
            cols = slice(t * 256, t * 256 + 256)
            out_ref[8 * f + t] = part_ref[f, :, cols]
            out_ref[24 + f, t : t + 1] = edge_ref[f, :, cols]


def pack(part, edge):
    return call(
        pack_kernel,
        vmem_out(27, 8, 256),
        in_vmem(part),
        in_vmem(edge),
        in_specs=[WHOLE] * 2,
        out_specs=WHOLE,
        name="pack",
    )


def mean_kernel(here_ref, there_ref, out_ref):
    out_ref[...] = (here_ref[...] + there_ref[...]) * (1.0 / 16.0)


def mean_of(here, there):
    return call(
        mean_kernel,
        vmem_out(*here.shape),
        in_vmem(here),
        in_vmem(there),
        in_specs=[WHOLE] * 2,
        out_specs=WHOLE,
        name="mean",
    )


def coeffs_kernel(where_ref, *refs):
    out_ref, mean, fields, sems = refs[8:]
    x, core = where_ref[0], where_ref[1]
    for k, piece in enumerate(refs[:8]):
        slot = (x + k) % 4
        side = core if k < 4 else 1 - core
        block = 1 + side * 4 + slot
        for f in range(3):
            for t in range(8):
                mean[f, block, :, t * 256 : t * 256 + 256] = piece[8 * f + t]

        @pl.when((side == 0) & (slot == 0))
        def _():
            for f in range(3):
                for t in range(8):
                    mean[f, 9, 0:1, t * 256 : t * 256 + 256] = piece[24 + f, t : t + 1]

        @pl.when((side == 1) & (slot == 3))
        def _():
            for f in range(3):
                for t in range(8):
                    mean[f, 0, 7:8, t * 256 : t * 256 + 256] = piece[24 + f, t : t + 1]

    copies = []
    for part in range(4):
        rows = pl.ds(part * 16, 16)
        for f in range(3):
            for r in (2 * part, 2 * part + 1):
                value = mean[f, r + 1]
                block = pl.ds(r * 8, 8)
                fields[f, block] = value + 1.0 if f == 2 else value
                fields[3 + 2 * f, block] = ddx(value)
                fields[4 + 2 * f, block] = ddy(mean[f, r], value, mean[f, r + 2])
            for planes in (pl.ds(f, 1), pl.ds(3 + 2 * f, 2)):
                copy = pltpu.make_async_copy(fields.at[planes, rows], out_ref.at[planes, rows], sems.at[len(copies)])
                copy.start()
                copies.append(copy)
    for copy in copies:
        copy.wait()


def coeffs_of(where, pieces, others, cols):
    return call(
        coeffs_kernel,
        jax.ShapeDtypeStruct((9, 64, cols), jnp.float32),
        where,
        *map(in_vmem, (*pieces, *others)),
        in_specs=[SCALARS] + [WHOLE] * 8,
        out_specs=pl.BlockSpec(memory_space=pl.ANY),
        scratch_shapes=[
            pltpu.VMEM((3, 10, 8, cols), jnp.float32),
            pltpu.VMEM((9, 64, cols), jnp.float32),
            pltpu.SemaphoreType.DMA((24,)),
        ],
        name="coeffs",
    )


def stage_kernel(state_ref, out_ref):
    out_ref[...] = state_ref[...]


def stage(state):
    return call(stage_kernel, vmem_out(*state.shape), state, in_specs=[WHOLE], out_specs=WHOLE, name="stage")


def local_kernel(which_ref, state_ref, above_ref, below_ref, other_ref, initial_ref, out_ref):
    def block(f, r):
        if r < 0:
            return jnp.broadcast_to(above_ref[f], (8, above_ref.shape[-1]))
        if r > 7:
            return jnp.broadcast_to(below_ref[f], (8, below_ref.shape[-1]))
        return state_ref[f, r]

    for r in range(8):
        u, v, e = (state_ref[f, r] for f in range(3))
        dx = [ddx(w) for w in (u, v, e)]
        dy = [ddy(block(f, r - 1), w, block(f, r + 1)) for f, w in enumerate((u, v, e))]
        force_u = -u * dx[0] - v * dy[0] + v - dx[2]
        force_v = -u * dx[1] - v * dy[1] - u - dy[2]
        depth = 1.0 + e
        force_e = -(depth * dx[0] + u * dx[2]) - (depth * dy[1] + v * dy[2])
        out_ref[0, r] = u - 0.5 * force_u
        out_ref[1, r] = v - 0.5 * force_v
        out_ref[2, r] = e - 0.5 * force_e

    @pl.when(which_ref[0] == 1)
    def _():
        out_ref[...] = out_ref[...] - other_ref[...]

    @pl.when(which_ref[0] == 2)
    def _():
        out_ref[...] = out_ref[...] - initial_ref[...]


def local_part(which, state, above, below, other, initial):
    cols = state.shape[-1]
    state, other, initial = (a.reshape(3, 8, 8, cols) for a in (state, other, initial))
    return call(
        local_kernel,
        vmem_out(3, 8, 8, cols),
        which,
        *map(in_vmem, (state, above, below, other, initial)),
        in_specs=[SCALARS] + [WHOLE] * 5,
        out_specs=WHOLE,
        name="local_part",
    ).reshape(3, 64, cols)


def residual_kernel(core_ref, local_ref, crossed_ref, stepped_ref, second_ref, out_ref, left, sems):
    first, second = slice(0, FIRST), slice(FIRST, 64)
    left[:, first] = local_ref[:, first] - stepped_ref[...]

    @pl.when(core_ref[0] == 0)
    def _():
        left[:, first] = left[:, first] - crossed_ref[...]

    copies = [pltpu.make_async_copy(left.at[:, first], out_ref.at[:, first], sems.at[0])]
    copies[0].start()
    left[:, second] = local_ref[:, second] - second_ref[...]
    copies.append(pltpu.make_async_copy(left.at[:, second], out_ref.at[:, second], sems.at[1]))
    copies[1].start()
    for copy in copies:
        copy.wait()


def residual_of(core, local, crossed, stepped, second):
    return call(
        residual_kernel,
        jax.ShapeDtypeStruct(local.shape, jnp.float32),
        core,
        *map(in_vmem, (local, crossed, stepped, second)),
        in_specs=[SCALARS] + [WHOLE] * 4,
        out_specs=pl.BlockSpec(memory_space=pl.ANY),
        scratch_shapes=[pltpu.VMEM(local.shape, jnp.float32), pltpu.SemaphoreType.DMA((2,))],
        name="residual",
    )


def shards(states, initial_state):
    current = states[0, 0]
    step, window = lax.axis_index("tm"), lax.axis_index("win")
    x, z_hi, core = step // 4, step // 2 % 2, step % 2
    where = jnp.stack([x, core]).astype(jnp.int32)

    other = send(current, swap_target)
    crossed = send(current[:, :FIRST], cross_first)
    held = stage(current)

    pieces = split_sum(where, held, other)
    above = send(after(held, pieces[0])[:, 63:64], up_target)
    below = send(after(held, pieces[0])[:, 0:1], down_target)
    came = [send(pieces[k], x_target(k)) for k in (1, 3, 2)]
    part = (pieces[0] + came[0]) + (came[1] + came[2])
    edge = jnp.where(core == 0, part[:, 0:1], part[:, 7:8])
    beside = send(edge, edge_target)

    second_half = after(held, edge)[:, FIRST:]
    shifted = send(second_half, step_first)
    stepped = send(after(crossed, edge), step_last)
    which = jnp.where(core == 1, 1, jnp.where((step == 0) & (window == 0), 2, 0)).astype(jnp.int32).reshape(1)
    local = local_part(which, after(held, edge), above, below, other, initial_state)

    part = pack(part, beside)
    part = mean_of(part, after(send(part, z_target), crossed, shifted, local))
    last = send(after(jnp.where(z_hi == 0, second_half, shifted), part), cross_last)
    gathered = [part] + [send(part, x_target(-k)) for k in (1, 2, 3)]
    others = [send(piece, swap_target) for piece in gathered]
    coeffs = coeffs_of(where, gathered, others, current.shape[-1])

    local = after(local, coeffs)
    residual = residual_of(core.astype(jnp.int32).reshape(1), local, crossed, stepped, last)
    return coeffs[None], residual[None, None]


def solution(mesh):
    in_specs = (P("win", "tm", None, "space", None), P(None, "space", None))
    out_specs = (P("win", None, "space", None), P("win", "tm", None, "space", None))
    return jax.shard_map(shards, mesh=mesh, in_specs=in_specs, out_specs=out_specs, check_vma=False)
```
